32 devices in a mesh: grp: 4 (over y, x), cell: 8 (over z, core).
Axes of the slice: x: 2, y: 2, z: 4, core: 2. Of those that a mesh axis runs over, the one named last changes fastest.
Arguments:
- occurrence: bfloat16 [98304, 4096], P(('grp', 'cell')), may hold values from 0 to 1, as said below
- condition: bfloat16 [98304], P(('grp', 'cell')), may hold values from 0.05 to 1, as said below
- neighbours: int32 [768, 4], P(('grp', 'cell')), may hold values from 0 to 767, as said below
- pair_count: int32 [768], P(('grp', 'cell')), may hold values from 0 to 4
Outputs:
- effective: float32 [98304], P(('grp', 'cell'))
- persistence: float32 [4096], P(('grp', 'cell'))
The draws below stay inside these ranges and needn't reach their ends.
Inputs may be any that keep to these rules, and one draw needn't show every extreme that they name: occurrence probabilities, positive. habitat condition, positive. `neighbours`: entry k of row t, for k < pair_count[t], is a tile u != t with |u - t| <= 2 in the same band of 192 consecutive tiles (t // 192 == u // 192); entries are distinct; pairing is symmetric (u lists t whenever t lists u); later entries hold t.
All inputs are finite; a program needn't handle non-finite values.
Results may differ from the reference program's by a relative error of at most 0.0003.
Values may be sent and summed in bfloat16 or wider, within the bound.
A program may use at most 384 MiB of HBM per device.

```python
import jax
import jax.numpy as jnp
from jax import lax

SPECIES = 4096
TILE = 128
RADIUS = 2
TILES_DEV = 24
GROUP_TILES = 192
TILES = 768
CELLS = 98304


def draw_occurrence(key, part):
    first, second, third, fourth = jax.random.split(key, 4)
    tile_of = jnp.arange(CELLS, dtype=jnp.int32) // TILE
    range_start = jax.random.randint(third, (SPECIES,), 0, TILES).astype(jnp.int32)
    range_span = (jax.random.randint(fourth, (SPECIES,), 1, 9) * TILES_DEV).astype(jnp.int32)
    inside = jnp.mod(tile_of[:, None] - range_start[None, :], TILES) < range_span[None, :]
    boost = jnp.where(inside, 7.0, 0.0)
    noise = jax.random.normal(first, (CELLS, SPECIES), jnp.float32) * 1.5
    richness = jax.random.uniform(second, (CELLS, 1), jnp.float32, -0.5, 0.5)
    logits = -6.0 + noise + richness + boost
    return jax.nn.sigmoid(logits).astype(jnp.bfloat16)


def draw_condition(key, part):
    first, second = jax.random.split(key, 2)
    regions = TILES // TILES_DEV
    level = jnp.exp(jax.random.uniform(first, (regions,), jnp.float32, -2.0, 0.0))
    rough = jnp.exp(jax.random.uniform(second, (CELLS,), jnp.float32, -0.7, 0.0))
    level_cells = jnp.repeat(level, TILES_DEV * TILE)
    return (level_cells * rough).astype(jnp.bfloat16)


def pair_lists(key):
    folded = jax.random.fold_in(key, 17)
    coins = jax.random.randint(folded, (TILES, RADIUS), 0, 2).astype(jnp.int32)
    own_tiles = jnp.arange(TILES, dtype=jnp.int32)
    position = own_tiles % GROUP_TILES
    coins = jnp.where(position[:, None] < 2 * RADIUS, 1, coins)
    steps_up = jnp.arange(1, RADIUS + 1, dtype=jnp.int32)
    upward = (coins == 1) & (position[:, None] + steps_up[None, :] < GROUP_TILES)
    downward = []
    for offset in range(RADIUS, 0, -1):
        moved = jnp.roll(upward[:, offset - 1], offset)
        downward.append(moved & (position >= offset))
    valid = jnp.concatenate([jnp.stack(downward, 1), upward], 1)
    candidate = jnp.concatenate([own_tiles[:, None] - steps_up[::-1][None, :], own_tiles[:, None] + steps_up[None, :]], 1)
    candidate = jnp.where(valid, candidate, own_tiles[:, None])
    slot_ids = jnp.arange(2 * RADIUS, dtype=jnp.int32)[None, :]
    ranking = jnp.where(valid, slot_ids, slot_ids + 2 * RADIUS)
    ordering = jnp.argsort(ranking, axis=1, stable=True)
    lists = jnp.take_along_axis(candidate, ordering, axis=1)
    counts = jnp.sum(valid.astype(jnp.int32), axis=1)
    return (lists.astype(jnp.int32), counts.astype(jnp.int32))


def draw_neighbours(key, part):
    return pair_lists(key)[0]


def draw_pair_count(key, part):
    return pair_lists(key)[1]


def setup_inputs(seed: int = 0) -> dict:
    streams_of = jax.random.split(jax.random.key(seed), 5)
    occurrence = draw_occurrence(jax.random.fold_in(streams_of[4], 71), 0)
    condition = draw_condition(jax.random.fold_in(streams_of[4], 71), 0)
    neighbours = draw_neighbours(jax.random.fold_in(streams_of[4], 71), 0)
    pair_count = draw_pair_count(jax.random.fold_in(streams_of[4], 71), 0)
    return {"occurrence": occurrence, "condition": condition, "neighbours": neighbours, "pair_count": pair_count}


sharpness = 40.0
epsilon = 1e-06
exponent = 0.25

def pair_hits(neighbours, counts, first_tile, radius):
    own_tiles = first_tile + jnp.arange(counts.shape[0], dtype=jnp.int32)
    live_slot = jnp.arange(neighbours.shape[1], dtype=jnp.int32)[None, :] < counts[:, None]
    offsets = jnp.arange(-radius, radius + 1, dtype=jnp.int32)
    hit_tile = (neighbours - own_tiles[:, None])[:, :, None] == offsets[None, None, :]
    matched = jnp.any(live_slot[:, :, None] & hit_tile, axis=1) | (offsets == 0)[None, :]
    return matched.astype(jnp.float32)

def band_weights(row_block, window, row_inv, win_inv, hits_rows, shift, lowest, radius):
    per_block = hits_rows.shape[0]
    col_tiles = window.shape[0] // TILE
    gram_block = lax.dot_general(row_block, window, (((1,), (1,)), ((), ())), preferred_element_type=jnp.float32)
    cosine = gram_block * row_inv[:, None] * win_inv[None, :]
    distance = jnp.arange(col_tiles, dtype=jnp.int32)[None, :] - shift - jnp.arange(per_block, dtype=jnp.int32)[:, None]
    inside = (distance >= lowest) & (distance <= radius)
    picked = jnp.take_along_axis(hits_rows, jnp.clip(distance + radius, 0, 2 * radius), axis=1)
    tiles_mask = jnp.where(inside, picked, 0.0)
    diagonal = jnp.eye(TILE, dtype=bool)
    selfpair = (distance == 0)[:, None, :, None] & diagonal[None, :, None, :]
    spread = jnp.broadcast_to(tiles_mask[:, None, :, None], (per_block, TILE, col_tiles, TILE))
    cellmask = jnp.where(selfpair, 0.0, spread).reshape(per_block * TILE, col_tiles * TILE)
    return jnp.exp(sharpness * cosine) * cellmask

def inverse_norms(block_rows):
    wide = block_rows.astype(jnp.float32)
    return lax.rsqrt(lax.optimization_barrier(jnp.sum(wide * wide, axis=1)) + epsilon)

def reference(occurrence, condition, neighbours, pair_count):
    hits = pair_hits(neighbours, pair_count, 0, RADIUS)
    per_block = 4
    margin = jnp.zeros((RADIUS * TILE, SPECIES), occurrence.dtype)
    padded = jnp.concatenate([margin, occurrence, margin], 0)
    cond_full = condition.astype(jnp.float32)
    cond_margin = jnp.zeros((RADIUS * TILE,), jnp.float32)
    cond_pad = jnp.concatenate([cond_margin, cond_full, cond_margin], 0)
    width = (per_block + 2 * RADIUS) * TILE

    def one_block(block_id):
        start = block_id * (per_block * TILE)
        row_block = lax.dynamic_slice_in_dim(occurrence, start, per_block * TILE, 0)
        window = lax.dynamic_slice_in_dim(padded, start, width, 0)
        cond_win = lax.dynamic_slice_in_dim(cond_pad, start, width, 0)
        cond_rows = lax.dynamic_slice_in_dim(cond_full, start, per_block * TILE, 0)
        hits_rows = lax.dynamic_slice_in_dim(hits, block_id * per_block, per_block, 0)
        weights = band_weights(row_block, window, inverse_norms(row_block), inverse_norms(window), hits_rows, RADIUS, -RADIUS, RADIUS)
        numer = lax.optimization_barrier(jnp.sum(weights * cond_win[None, :], axis=1))
        denom = lax.optimization_barrier(jnp.sum(weights, axis=1))
        return cond_rows * numer / denom
    effective = lax.map(one_block, jnp.arange(TILES // per_block, dtype=jnp.int32)).reshape(CELLS)
    weighted = jnp.stack([effective.astype(jnp.bfloat16), jnp.ones((CELLS,), jnp.float32).astype(jnp.bfloat16)])
    totals = jnp.dot(weighted, occurrence, preferred_element_type=jnp.float32)
    persistence = (totals[0] / totals[1]) ** exponent
    return (effective, persistence)
```

```python
import functools
import math

import jax
import jax.numpy as jnp
from jax import lax
from jax.experimental import pallas as pl
from jax.experimental.pallas import tpu as pltpu
from jax.sharding import PartitionSpec as P

sharpness = 40.0
epsilon = 1e-06
exponent = 0.25

TILE = 128
PAIR = 2 * TILE
SCALE = sharpness * math.log2(math.e)


def gram_dot(a, b):
    return lax.dot_general(a, b, (((1,), (1,)), ((), ())), preferred_element_type=jnp.float32)


def fold_rows(x):
    return jnp.sum(x.reshape(x.shape[0] // 8, 8, x.shape[1]), axis=0)


def main_kernel(
    n_cell, tiles, occ_hbm, cond_ref, nb_ref, cnt_ref, eff_ref, sums_ref,
    ext, gram_a, gram_b, irow, icol, crow, ccol, acc, xin, wl,
    load_sem, halo_send, halo_recv, cond_send, cond_recv, acc_send, acc_recv,
):
    rows = tiles * TILE
    pairs = tiles // 2 + 1
    last = pairs - 1
    ext_rows = rows + PAIR
    species = ext.shape[1]
    me = lax.axis_index("cell")
    first_tile = (lax.axis_index("grp") * n_cell + me) * tiles
    has_left = me > 0
    has_right = me < n_cell - 1
    left = {"cell": jnp.maximum(me - 1, 0)}
    right = {"cell": jnp.minimum(me + 1, n_cell - 1)}
    mesh_id = pl.DeviceIdType.MESH

    def load(k):
        lo, hi = max(k * PAIR, TILE), min((k + 1) * PAIR, ext_rows - TILE)
        return pltpu.make_async_copy(
            occ_hbm.at[pl.ds(lo - TILE, hi - lo)], ext.at[pl.ds(lo, hi - lo)], load_sem.at[k]
        )

    for k in list(range(1, last)) + [0, last]:
        load(k).start()

    for t in range(tiles):
        crow[t + 1] = jnp.broadcast_to(cond_ref[t : t + 1, :], (8, TILE))

    barrier = pltpu.get_barrier_semaphore()

    @pl.when(has_left)
    def _():
        pl.semaphore_signal(barrier, inc=1, device_id=left, device_id_type=mesh_id)

    @pl.when(has_right)
    def _():
        pl.semaphore_signal(barrier, inc=1, device_id=right, device_id_type=mesh_id)

    pl.semaphore_wait(barrier, has_left.astype(jnp.int32) + has_right.astype(jnp.int32))

    def remote(src, dst, send, recv, slot, target):
        return pltpu.make_async_remote_copy(
            src_ref=src, dst_ref=dst, send_sem=send.at[slot], recv_sem=recv.at[slot],
            device_id=target, device_id_type=mesh_id,
        )

    halo_r = remote(
        occ_hbm.at[pl.ds(rows - TILE, TILE)], ext.at[pl.ds(0, TILE)], halo_send, halo_recv, 0, right
    )
    halo_l = remote(
        occ_hbm.at[pl.ds(0, TILE)], ext.at[pl.ds(ext_rows - TILE, TILE)], halo_send, halo_recv, 1, left
    )
    cond_r = remote(crow.at[tiles], crow.at[0], cond_send, cond_recv, 0, right)
    cond_l = remote(crow.at[1], crow.at[tiles + 1], cond_send, cond_recv, 1, left)
    acc_r = remote(acc.at[tiles + 1], xin.at[0], acc_send, acc_recv, 0, right)
    acc_l = remote(acc.at[0], xin.at[1], acc_send, acc_recv, 1, left)

    @pl.when(has_right)
    def _():
        halo_r.start()
        cond_r.start()

    @pl.when(has_left)
    def _():
        halo_l.start()
        cond_l.start()

    @pl.when(jnp.logical_not(has_left))
    def _():
        ext[pl.ds(0, TILE), :] = jnp.zeros((TILE, species), ext.dtype)
        crow[0] = jnp.zeros((8, TILE), jnp.float32)
        xin[0] = jnp.zeros((16, TILE), jnp.float32)

    @pl.when(jnp.logical_not(has_right))
    def _():
        ext[pl.ds(ext_rows - TILE, TILE), :] = jnp.zeros((TILE, species), ext.dtype)
        crow[tiles + 1] = jnp.zeros((8, TILE), jnp.float32)
        xin[1] = jnp.zeros((16, TILE), jnp.float32)

    def column(row8):
        return jnp.transpose(jnp.broadcast_to(row8[0:1, :], (TILE, TILE)))

    for e in range(1, tiles + 1):
        ccol[e] = column(crow[e])

    def hit(t, offset):
        wanted = first_tile + t + offset
        found = jnp.int32(0)
        for s in range(nb_ref.shape[1]):
            same = jnp.logical_and(nb_ref[t, s] == wanted, s < cnt_ref[t])
            found = jnp.maximum(found, same.astype(jnp.int32))
        return found.astype(jnp.float32)

    eye = lax.broadcasted_iota(jnp.int32, (TILE, TILE), 0) == lax.broadcasted_iota(
        jnp.int32, (TILE, TILE), 1
    )

    def part(ref, base, i, j):
        return ref[base + i * TILE : base + (i + 1) * TILE, j * TILE : (j + 1) * TILE]

    def own_own(ref, base, k, near, guest=None):
        e = 2 * k
        tiles_g = [[part(ref, base, i, j) for j in range(2)] for i in range(2)]
        rows_inv = []
        cols_inv = []
        for i in range(2):
            diag = jnp.sum(jnp.where(eye, tiles_g[i][i], 0.0), axis=0, keepdims=True)
            inv = jnp.broadcast_to(lax.rsqrt(diag + epsilon), (TILE, TILE))
            col = jnp.transpose(inv) * SCALE
            irow[e + i] = inv[0:8]
            icol[e + i] = col
            rows_inv.append(inv[0:1])
            cols_inv.append(col)
        cc = [ccol[e], ccol[e + 1]]
        w = [[None, None], [None, None]]
        for i in range(2):
            for j in range(2):
                v = jnp.exp2(tiles_g[i][j] * cols_inv[i] * rows_inv[j])
                if i == j and i == guest:
                    w[i][j] = jnp.zeros_like(v)
                elif i == j:
                    w[i][j] = jnp.where(eye, 0.0, v)
                else:
                    w[i][j] = v if near is None else v * near
        for j in range(2):
            if near is None:
                numer, denom = w[j][j] * cc[j], w[j][j]
            else:
                numer, denom = w[0][j] * cc[0] + w[1][j] * cc[1], w[0][j] + w[1][j]
            acc[e + j, 0:8, :] = fold_rows(numer)
            acc[e + j, 8:16, :] = fold_rows(denom)

    def prev_own(ref, base, k, far0, near1, far1):
        e = 2 * k
        r0, r1 = irow[e, 0:1, :], irow[e + 1, 0:1, :]
        w00 = jnp.exp2(part(ref, base, 0, 0) * icol[e - 2] * r0) * far0
        w10 = jnp.exp2(part(ref, base, 1, 0) * icol[e - 1] * r0) * near1
        w11 = jnp.exp2(part(ref, base, 1, 1) * icol[e - 1] * r1) * far1
        cp0, cp1 = ccol[e - 2], ccol[e - 1]
        acc[e, 0:8, :] += fold_rows(w00 * cp0 + w10 * cp1)
        acc[e, 8:16, :] += fold_rows(w00 + w10)
        acc[e + 1, 0:8, :] += fold_rows(w11 * cp1)
        acc[e + 1, 8:16, :] += fold_rows(w11)
        c0, c1 = crow[e, 0:1, :], crow[e + 1, 0:1, :]
        acc[e - 2, 0:8, :] += fold_rows(jnp.transpose(w00 * c0))
        acc[e - 2, 8:16, :] += fold_rows(jnp.transpose(w00))
        acc[e - 1, 0:8, :] += fold_rows(jnp.transpose(w10 * c0 + w11 * c1))
        acc[e - 1, 8:16, :] += fold_rows(jnp.transpose(w10 + w11))

    def pair_rows(k, count=1):
        start = k * PAIR
        if not isinstance(k, int):
            start = pl.multiple_of(start, PAIR)
        return ext[pl.ds(start, count * PAIR), :]

    def block(k, ref):
        ref[...] = gram_dot(pair_rows(k - 1, 2), pair_rows(k))

    def block_post(k, ref):
        own_own(ref, PAIR, k, hit(2 * k - 1, 1))
        prev_own(ref, 0, k, hit(2 * k - 3, 2), hit(2 * k - 2, 1), hit(2 * k - 2, 2))

    def wait_load(k):
        start = pl.multiple_of(k * PAIR, PAIR)
        pltpu.make_async_copy(
            occ_hbm.at[pl.ds(start - TILE, PAIR)], ext.at[pl.ds(start, PAIR)], load_sem.at[k]
        ).wait()

    load(1).wait()
    gram_b[0:PAIR, :] = gram_dot(pair_rows(1), pair_rows(1))
    load(2).wait()
    block(2, gram_a)
    own_own(gram_b, 0, 1, hit(1, 1))

    def two(i, carry):
        k = 2 * i + 3
        wait_load(k)
        block(k, gram_b)
        block_post(k - 1, gram_a)
        wait_load(k + 1)
        block(k + 1, gram_a)
        block_post(k, gram_b)
        return carry

    steps = (last - 3) // 2
    lax.fori_loop(0, steps, two, 0)
    tail = 2 * steps + 3
    current = gram_a
    for k in range(tail, last):
        other = gram_b if current is gram_a else gram_a
        load(k).wait()
        block(k, other)
        block_post(k - 1, current)
        current = other

    load(0).wait()
    load(last).wait()
    other = gram_b if current is gram_a else gram_a

    @pl.when(has_left)
    def _():
        halo_r.wait_recv()
        cond_r.wait_recv()

    @pl.when(has_right)
    def _():
        halo_l.wait_recv()
        cond_l.wait_recv()

    ccol[0] = column(crow[0])
    ccol[tiles + 1] = column(crow[tiles + 1])
    other[0:PAIR, :] = gram_dot(pair_rows(0), pair_rows(0))
    other[PAIR:, :] = gram_dot(pair_rows(0), pair_rows(1))
    block_post(last - 1, current)
    block(last, current)
    own_own(other, 0, 0, hit(0, -1), 0)
    prev_own(other, PAIR, 1, hit(1, -2), hit(0, 1), hit(0, 2))
    own_own(current, PAIR, last, None, 1)
    prev_own(current, 0, last, hit(tiles - 3, 2), hit(tiles - 2, 1), hit(tiles - 2, 2))

    @pl.when(has_right)
    def _():
        acc_r.start()

    @pl.when(has_left)
    def _():
        acc_l.start()

    line = lax.broadcasted_iota(jnp.int32, (16, TILE), 0)

    def finish(t, extra):
        e = t + 1
        total = acc[e]
        if extra is not None:
            total = total + xin[extra]
        numer = jnp.sum(total[0:8], axis=0, keepdims=True)
        denom = jnp.sum(total[8:16], axis=0, keepdims=True)
        eff = crow[e, 0:1, :] * numer / denom
        eff_ref[t : t + 1, :] = eff
        both = jnp.where(line == 0, eff, jnp.where(line == 1, 1.0, 0.0))
        wl[:, t * TILE : (t + 1) * TILE] = both.astype(jnp.bfloat16)

    for t in range(1, tiles - 1):
        finish(t, None)

    step = 512 if species % 512 == 0 else TILE

    def inner(i, carry):
        cols = pl.ds(pl.multiple_of(i * step, step), step)
        got = jnp.dot(
            wl[:, TILE : rows - TILE], ext[PAIR : rows, cols], preferred_element_type=jnp.float32
        )
        sums_ref[:, cols] = got[0:8]
        return carry

    lax.fori_loop(0, species // step, inner, 0)

    @pl.when(has_left)
    def _():
        acc_r.wait_recv()

    @pl.when(has_right)
    def _():
        acc_l.wait_recv()

    finish(0, 0)
    finish(tiles - 1, 1)

    def outer(i, carry):
        cols = pl.ds(pl.multiple_of(i * step, step), step)
        got = jnp.dot(
            wl[:, 0:TILE], ext[TILE:PAIR, cols], preferred_element_type=jnp.float32
        ) + jnp.dot(
            wl[:, rows - TILE : rows], ext[rows : rows + TILE, cols],
            preferred_element_type=jnp.float32,
        )
        sums_ref[:, cols] += got[0:8]
        return carry

    lax.fori_loop(0, species // step, outer, 0)

    @pl.when(has_right)
    def _():
        halo_r.wait_send()
        cond_r.wait_send()
        acc_r.wait_send()

    @pl.when(has_left)
    def _():
        halo_l.wait_send()
        cond_l.wait_send()
        acc_l.wait_send()


def per_device(n_cell, occurrence, condition, neighbours, pair_count):
    tiles = pair_count.shape[0]
    rows, species = occurrence.shape
    cond = condition.astype(jnp.float32).reshape(tiles, TILE)
    vmem = pl.BlockSpec(memory_space=pltpu.VMEM)
    smem = pl.BlockSpec(memory_space=pltpu.SMEM)
    effective, sums = pl.pallas_call(
        functools.partial(main_kernel, n_cell, tiles),
        out_shape=(
            jax.ShapeDtypeStruct((tiles, TILE), jnp.float32),
            jax.ShapeDtypeStruct((8, species), jnp.float32),
        ),
        in_specs=[pl.BlockSpec(memory_space=pl.ANY), vmem, smem, smem],
        out_specs=(vmem, vmem),
        scratch_shapes=[
            pltpu.VMEM((rows + PAIR, species), jnp.bfloat16),
            pltpu.VMEM((2 * PAIR, PAIR), jnp.float32),
            pltpu.VMEM((2 * PAIR, PAIR), jnp.float32),
            pltpu.VMEM((tiles + 2, 8, TILE), jnp.float32),
            pltpu.VMEM((tiles + 2, TILE, TILE), jnp.float32),
            pltpu.VMEM((tiles + 2, 8, TILE), jnp.float32),
            pltpu.VMEM((tiles + 2, TILE, TILE), jnp.float32),
            pltpu.VMEM((tiles + 2, 16, TILE), jnp.float32),
            pltpu.VMEM((2, 16, TILE), jnp.float32),
            pltpu.VMEM((16, rows), jnp.bfloat16),
            pltpu.SemaphoreType.DMA((tiles // 2 + 1,)),
            pltpu.SemaphoreType.DMA((2,)),
            pltpu.SemaphoreType.DMA((2,)),
            pltpu.SemaphoreType.DMA((2,)),
            pltpu.SemaphoreType.DMA((2,)),
            pltpu.SemaphoreType.DMA((2,)),
            pltpu.SemaphoreType.DMA((2,)),
        ],
        compiler_params=pltpu.CompilerParams(
            collective_id=0, has_side_effects=True, vmem_limit_bytes=56 * 2**20
        ),
    )(occurrence, cond, neighbours, pair_count)
    totals = lax.psum_scatter(sums[0:2], ("grp", "cell"), scatter_dimension=1, tiled=True)
    persistence = (totals[0] / totals[1]) ** exponent
    return effective.reshape(rows), persistence


def solution(mesh):
    return jax.shard_map(
        functools.partial(per_device, mesh.shape["cell"]),
        mesh=mesh,
        in_specs=(
            P(("grp", "cell"), None),
            P(("grp", "cell")),
            P(("grp", "cell"), None),
            P(("grp", "cell")),
        ),
        out_specs=(P(("grp", "cell")), P(("grp", "cell"))),
        check_vma=False,
    )
```

```python
import functools
import math

import jax
import jax.numpy as jnp
from jax import lax
from jax.experimental import pallas as pl
from jax.experimental.pallas import tpu as pltpu
from jax.sharding import PartitionSpec as P

sharpness = 40.0
epsilon = 1e-06
exponent = 0.25

TILE = 128
PAIR = 2 * TILE
SCALE = sharpness * math.log2(math.e)


def gram_dot(a, b):
    return lax.dot_general(a, b, (((1,), (1,)), ((), ())), preferred_element_type=jnp.float32)


def fold_rows(x):
    return jnp.sum(x.reshape(x.shape[0] // 8, 8, x.shape[1]), axis=0)


def main_kernel(
    n_cell, tiles, occ_hbm, cond_ref, nb_ref, cnt_ref, eff_ref, sums_ref,
    ext, gram_a, gram_b, irow, icol, crow, ccol, acc, xin, wl,
    load_sem, halo_send, halo_recv, cond_send, cond_recv, acc_send, acc_recv,
):
    rows = tiles * TILE
    pairs = tiles // 2 + 1
    last = pairs - 1
    ext_rows = rows + PAIR
    species = ext.shape[1]
    me = lax.axis_index("cell")
    first_tile = (lax.axis_index("grp") * n_cell + me) * tiles
    has_left = me > 0
    has_right = me < n_cell - 1
    left = {"cell": jnp.maximum(me - 1, 0)}
    right = {"cell": jnp.minimum(me + 1, n_cell - 1)}
    mesh_id = pl.DeviceIdType.MESH

    def load(k):
        lo, hi = max(k * PAIR, TILE), min((k + 1) * PAIR, ext_rows - TILE)
        return pltpu.make_async_copy(
            occ_hbm.at[pl.ds(lo - TILE, hi - lo)], ext.at[pl.ds(lo, hi - lo)], load_sem.at[k]
        )

    for k in list(range(1, last)) + [0, last]:
        load(k).start()

    for t in range(tiles):
        crow[t + 1] = jnp.broadcast_to(cond_ref[t : t + 1, :], (8, TILE))

    barrier = pltpu.get_barrier_semaphore()

    @pl.when(has_left)
    def _():
        pl.semaphore_signal(barrier, inc=1, device_id=left, device_id_type=mesh_id)

    @pl.when(has_right)
    def _():
        pl.semaphore_signal(barrier, inc=1, device_id=right, device_id_type=mesh_id)

    pl.semaphore_wait(barrier, has_left.astype(jnp.int32) + has_right.astype(jnp.int32))

    def remote(src, dst, send, recv, slot, target):
        return pltpu.make_async_remote_copy(
            src_ref=src, dst_ref=dst, send_sem=send.at[slot], recv_sem=recv.at[slot],
            device_id=target, device_id_type=mesh_id,
        )

    halo_r = remote(
        occ_hbm.at[pl.ds(rows - TILE, TILE)], ext.at[pl.ds(0, TILE)], halo_send, halo_recv, 0, right
    )
    halo_l = remote(
        occ_hbm.at[pl.ds(0, TILE)], ext.at[pl.ds(ext_rows - TILE, TILE)], halo_send, halo_recv, 1, left
    )
    cond_r = remote(crow.at[tiles], crow.at[0], cond_send, cond_recv, 0, right)
    cond_l = remote(crow.at[1], crow.at[tiles + 1], cond_send, cond_recv, 1, left)
    acc_r = remote(acc.at[tiles + 1], xin.at[0], acc_send, acc_recv, 0, right)
    acc_l = remote(acc.at[0], xin.at[1], acc_send, acc_recv, 1, left)

    @pl.when(has_right)
    def _():
        halo_r.start()
        cond_r.start()

    @pl.when(has_left)
    def _():
        halo_l.start()
        cond_l.start()

    @pl.when(jnp.logical_not(has_left))
    def _():
        ext[pl.ds(0, TILE), :] = jnp.zeros((TILE, species), ext.dtype)
        crow[0] = jnp.zeros((8, TILE), jnp.float32)
        xin[0] = jnp.zeros((16, TILE), jnp.float32)

    @pl.when(jnp.logical_not(has_right))
    def _():
        ext[pl.ds(ext_rows - TILE, TILE), :] = jnp.zeros((TILE, species), ext.dtype)
        crow[tiles + 1] = jnp.zeros((8, TILE), jnp.float32)
        xin[1] = jnp.zeros((16, TILE), jnp.float32)

    def column(row8):
        return jnp.transpose(jnp.broadcast_to(row8[0:1, :], (TILE, TILE)))

    for e in range(1, tiles + 1):
        ccol[e] = column(crow[e])

    def hit(t, offset):
        wanted = first_tile + t + offset
        found = jnp.int32(0)
        for s in range(nb_ref.shape[1]):
            same = jnp.logical_and(nb_ref[t, s] == wanted, s < cnt_ref[t])
            found = jnp.maximum(found, same.astype(jnp.int32))
        return found.astype(jnp.float32)

    eye = lax.broadcasted_iota(jnp.int32, (TILE, TILE), 0) == lax.broadcasted_iota(
        jnp.int32, (TILE, TILE), 1
    )

    def part(ref, base, i, j):
        return ref[base + i * TILE : base + (i + 1) * TILE, j * TILE : (j + 1) * TILE]

    def own_own(ref, base, k, near, guest=None):
        e = 2 * k
        tiles_g = [[part(ref, base, i, j) for j in range(2)] for i in range(2)]
        rows_inv = []
        cols_inv = []
        for i in range(2):
            diag = jnp.sum(jnp.where(eye, tiles_g[i][i], 0.0), axis=0, keepdims=True)
            inv = jnp.broadcast_to(lax.rsqrt(diag + epsilon), (TILE, TILE))
            col = jnp.transpose(inv) * SCALE
            irow[e + i] = inv[0:8]
            icol[e + i] = col
            rows_inv.append(inv[0:1])
            cols_inv.append(col)
        cc = [ccol[e], ccol[e + 1]]
        w = [[None, None], [None, None]]
        for i in range(2):
            for j in range(2):
                v = jnp.exp2(tiles_g[i][j] * cols_inv[i] * rows_inv[j])
                if i == j and i == guest:
                    w[i][j] = jnp.zeros_like(v)
                elif i == j:
                    w[i][j] = jnp.where(eye, 0.0, v)
                else:
                    w[i][j] = v if near is None else v * near
        for j in range(2):
            if near is None:
                numer, denom = w[j][j] * cc[j], w[j][j]
            else:
                numer, denom = w[0][j] * cc[0] + w[1][j] * cc[1], w[0][j] + w[1][j]
            acc[e + j, 0:8, :] = fold_rows(numer)
            acc[e + j, 8:16, :] = fold_rows(denom)

    def prev_own(ref, base, k, far0, near1, far1):
        e = 2 * k
        r0, r1 = irow[e, 0:1, :], irow[e + 1, 0:1, :]
        w00 = jnp.exp2(part(ref, base, 0, 0) * icol[e - 2] * r0) * far0
        w10 = jnp.exp2(part(ref, base, 1, 0) * icol[e - 1] * r0) * near1
        w11 = jnp.exp2(part(ref, base, 1, 1) * icol[e - 1] * r1) * far1
        cp0, cp1 = ccol[e - 2], ccol[e - 1]
        acc[e, 0:8, :] += fold_rows(w00 * cp0 + w10 * cp1)
        acc[e, 8:16, :] += fold_rows(w00 + w10)
        acc[e + 1, 0:8, :] += fold_rows(w11 * cp1)
        acc[e + 1, 8:16, :] += fold_rows(w11)
        c0, c1 = crow[e, 0:1, :], crow[e + 1, 0:1, :]
        acc[e - 2, 0:8, :] += fold_rows(jnp.transpose(w00 * c0))
        acc[e - 2, 8:16, :] += fold_rows(jnp.transpose(w00))
        acc[e - 1, 0:8, :] += fold_rows(jnp.transpose(w10 * c0 + w11 * c1))
        acc[e - 1, 8:16, :] += fold_rows(jnp.transpose(w10 + w11))

    def pair_rows(k, count=1):
        start = k * PAIR
        if not isinstance(k, int):
            start = pl.multiple_of(start, PAIR)
        return ext[pl.ds(start, count * PAIR), :]

    def block(k, ref):
        ref[...] = gram_dot(pair_rows(k - 1, 2), pair_rows(k))

    def block_post(k, ref):
        own_own(ref, PAIR, k, hit(2 * k - 1, 1))
        prev_own(ref, 0, k, hit(2 * k - 3, 2), hit(2 * k - 2, 1), hit(2 * k - 2, 2))

    def wait_load(k):
        start = pl.multiple_of(k * PAIR, PAIR)
        pltpu.make_async_copy(
            occ_hbm.at[pl.ds(start - TILE, PAIR)], ext.at[pl.ds(start, PAIR)], load_sem.at[k]
        ).wait()

    load(1).wait()
    gram_b[0:PAIR, :] = gram_dot(pair_rows(1), pair_rows(1))
    load(2).wait()
    block(2, gram_a)
    own_own(gram_b, 0, 1, hit(1, 1))

    def two(i, carry):
        k = 2 * i + 3
        wait_load(k)
        block(k, gram_b)
        block_post(k - 1, gram_a)
        wait_load(k + 1)
        block(k + 1, gram_a)
        block_post(k, gram_b)
        return carry

    steps = (last - 3) // 2
    lax.fori_loop(0, steps, two, 0)
    tail = 2 * steps + 3
    current = gram_a
    for k in range(tail, last):
        other = gram_b if current is gram_a else gram_a
        load(k).wait()
        block(k, other)
        block_post(k - 1, current)
        current = other

    load(0).wait()
    load(last).wait()
    other = gram_b if current is gram_a else gram_a

    @pl.when(has_left)
    def _():
        halo_r.wait_recv()
        cond_r.wait_recv()

    @pl.when(has_right)
    def _():
        halo_l.wait_recv()
        cond_l.wait_recv()

    ccol[0] = column(crow[0])
    ccol[tiles + 1] = column(crow[tiles + 1])
    other[0:PAIR, :] = gram_dot(pair_rows(0), pair_rows(0))
    other[PAIR:, :] = gram_dot(pair_rows(0), pair_rows(1))
    block_post(last - 1, current)
    block(last, current)
    own_own(other, 0, 0, hit(0, -1), 0)
    prev_own(other, PAIR, 1, hit(1, -2), hit(0, 1), hit(0, 2))
    own_own(current, PAIR, last, None, 1)
    prev_own(current, 0, last, hit(tiles - 3, 2), hit(tiles - 2, 1), hit(tiles - 2, 2))

    @pl.when(has_right)
    def _():
        acc_r.start()

    @pl.when(has_left)
    def _():
        acc_l.start()

    line = lax.broadcasted_iota(jnp.int32, (16, TILE), 0)

    def finish(t, extra):
        e = t + 1
        total = acc[e]
        if extra is not None:
            total = total + xin[extra]
        numer = jnp.sum(total[0:8], axis=0, keepdims=True)
        denom = jnp.sum(total[8:16], axis=0, keepdims=True)
        eff = crow[e, 0:1, :] * numer / denom
        eff_ref[t : t + 1, :] = eff
        both = jnp.where(line == 0, eff, jnp.where(line == 1, 1.0, 0.0))
        wl[:, t * TILE : (t + 1) * TILE] = both.astype(jnp.bfloat16)

    for t in range(1, tiles - 1):
        finish(t, None)

    step = 512 if species % 512 == 0 else TILE

    def inner(i, carry):
        cols = pl.ds(pl.multiple_of(i * step, step), step)
        got = jnp.dot(
            wl[:, TILE : rows - TILE], ext[PAIR : rows, cols], preferred_element_type=jnp.float32
        )
        sums_ref[:, cols] = got[0:8]
        return carry

    lax.fori_loop(0, species // step, inner, 0)

    @pl.when(has_left)
    def _():
        acc_r.wait_recv()

    @pl.when(has_right)
    def _():
        acc_l.wait_recv()

    finish(0, 0)
    finish(tiles - 1, 1)

    def outer(i, carry):
        cols = pl.ds(pl.multiple_of(i * step, step), step)
        got = jnp.dot(
            wl[:, 0:TILE], ext[TILE:PAIR, cols], preferred_element_type=jnp.float32
        ) + jnp.dot(
            wl[:, rows - TILE : rows], ext[rows : rows + TILE, cols],
            preferred_element_type=jnp.float32,
        )
        sums_ref[:, cols] += got[0:8]
        return carry

    lax.fori_loop(0, species // step, outer, 0)

    @pl.when(has_right)
    def _():
        halo_r.wait_send()
        cond_r.wait_send()
        acc_r.wait_send()

    @pl.when(has_left)
    def _():
        halo_l.wait_send()
        cond_l.wait_send()
        acc_l.wait_send()


def per_device(n_cell, occurrence, condition, neighbours, pair_count):
    tiles = pair_count.shape[0]
    rows, species = occurrence.shape
    cond = condition.astype(jnp.float32).reshape(tiles, TILE)
    vmem = pl.BlockSpec(memory_space=pltpu.VMEM)
    smem = pl.BlockSpec(memory_space=pltpu.SMEM)
    effective, sums = pl.pallas_call(
        functools.partial(main_kernel, n_cell, tiles),
        out_shape=(
            jax.ShapeDtypeStruct((tiles, TILE), jnp.float32),
            jax.ShapeDtypeStruct((8, species), jnp.float32),
        ),
        in_specs=[pl.BlockSpec(memory_space=pl.ANY), vmem, smem, smem],
        out_specs=(vmem, vmem),
        scratch_shapes=[
            pltpu.VMEM((rows + PAIR, species), jnp.bfloat16),
            pltpu.VMEM((2 * PAIR, PAIR), jnp.float32),
            pltpu.VMEM((2 * PAIR, PAIR), jnp.float32),
            pltpu.VMEM((tiles + 2, 8, TILE), jnp.float32),
            pltpu.VMEM((tiles + 2, TILE, TILE), jnp.float32),
            pltpu.VMEM((tiles + 2, 8, TILE), jnp.float32),
            pltpu.VMEM((tiles + 2, TILE, TILE), jnp.float32),
            pltpu.VMEM((tiles + 2, 16, TILE), jnp.float32),
            pltpu.VMEM((2, 16, TILE), jnp.float32),
            pltpu.VMEM((16, rows), jnp.bfloat16),
            pltpu.SemaphoreType.DMA((tiles // 2 + 1,)),
            pltpu.SemaphoreType.DMA((2,)),
            pltpu.SemaphoreType.DMA((2,)),
            pltpu.SemaphoreType.DMA((2,)),
            pltpu.SemaphoreType.DMA((2,)),
            pltpu.SemaphoreType.DMA((2,)),
            pltpu.SemaphoreType.DMA((2,)),
        ],
        compiler_params=pltpu.CompilerParams(
            collective_id=0, has_side_effects=True, vmem_limit_bytes=56 * 2**20
        ),
    )(occurrence, cond, neighbours, pair_count)
    axes = ("grp", "cell")
    owners = lax.axis_size(axes)
    blocks = jnp.transpose(sums[0:2].reshape(2, owners, species // owners), (1, 0, 2))
    totals = jnp.sum(lax.all_to_all(blocks, axes, 0, 0, tiled=True), axis=0)
    persistence = (totals[0] / totals[1]) ** exponent
    return effective.reshape(rows), persistence


def solution(mesh):
    return jax.shard_map(
        functools.partial(per_device, mesh.shape["cell"]),
        mesh=mesh,
        in_specs=(
            P(("grp", "cell"), None),
            P(("grp", "cell")),
            P(("grp", "cell"), None),
            P(("grp", "cell")),
        ),
        out_specs=(P(("grp", "cell")), P(("grp", "cell"))),
        check_vma=False,
    )
```

```python
import functools
import math

import jax
import jax.numpy as jnp
from jax import lax
from jax.experimental import pallas as pl
from jax.experimental.pallas import tpu as pltpu
from jax.sharding import PartitionSpec as P

sharpness = 40.0
epsilon = 1e-06
exponent = 0.25

TILE = 128
PAIR = 2 * TILE
SCALE = sharpness * math.log2(math.e)


def gram_dot(a, b):
    return lax.dot_general(a, b, (((1,), (1,)), ((), ())), preferred_element_type=jnp.float32)


def fold_rows(x):
    return jnp.sum(x.reshape(x.shape[0] // 8, 8, x.shape[1]), axis=0)


def main_kernel(
    n_cell, tiles, occ_hbm, cond_ref, nb_ref, cnt_ref, eff_ref, sums_ref,
    ext, gram_a, gram_b, irow, icol, crow, ccol, acc, xin, wl,
    load_sem, halo_send, halo_recv, cond_send, cond_recv, acc_send, acc_recv,
):
    rows = tiles * TILE
    pairs = tiles // 2 + 1
    last = pairs - 1
    ext_rows = rows + PAIR
    species = ext.shape[1]
    me = lax.axis_index("cell")
    first_tile = (lax.axis_index("grp") * n_cell + me) * tiles
    has_left = me > 0
    has_right = me < n_cell - 1
    left = {"cell": jnp.maximum(me - 1, 0)}
    right = {"cell": jnp.minimum(me + 1, n_cell - 1)}
    mesh_id = pl.DeviceIdType.MESH

    def load(k):
        lo, hi = max(k * PAIR, TILE), min((k + 1) * PAIR, ext_rows - TILE)
        return pltpu.make_async_copy(
            occ_hbm.at[pl.ds(lo - TILE, hi - lo)], ext.at[pl.ds(lo, hi - lo)], load_sem.at[k]
        )

    for k in list(range(1, last)) + [0, last]:
        load(k).start()

    for t in range(tiles):
        crow[t + 1] = jnp.broadcast_to(cond_ref[t : t + 1, :], (8, TILE))

    barrier = pltpu.get_barrier_semaphore()

    @pl.when(has_left)
    def _():
        pl.semaphore_signal(barrier, inc=1, device_id=left, device_id_type=mesh_id)

    @pl.when(has_right)
    def _():
        pl.semaphore_signal(barrier, inc=1, device_id=right, device_id_type=mesh_id)

    pl.semaphore_wait(barrier, has_left.astype(jnp.int32) + has_right.astype(jnp.int32))

    def remote(src, dst, send, recv, slot, target):
        return pltpu.make_async_remote_copy(
            src_ref=src, dst_ref=dst, send_sem=send.at[slot], recv_sem=recv.at[slot],
            device_id=target, device_id_type=mesh_id,
        )

    halo_r = remote(
        occ_hbm.at[pl.ds(rows - TILE, TILE)], ext.at[pl.ds(0, TILE)], halo_send, halo_recv, 0, right
    )
    halo_l = remote(
        occ_hbm.at[pl.ds(0, TILE)], ext.at[pl.ds(ext_rows - TILE, TILE)], halo_send, halo_recv, 1, left
    )
    cond_r = remote(crow.at[tiles], crow.at[0], cond_send, cond_recv, 0, right)
    cond_l = remote(crow.at[1], crow.at[tiles + 1], cond_send, cond_recv, 1, left)
    acc_r = remote(acc.at[tiles + 1], xin.at[0], acc_send, acc_recv, 0, right)
    acc_l = remote(acc.at[0], xin.at[1], acc_send, acc_recv, 1, left)

    @pl.when(has_right)
    def _():
        halo_r.start()
        cond_r.start()

    @pl.when(has_left)
    def _():
        halo_l.start()
        cond_l.start()

    @pl.when(jnp.logical_not(has_left))
    def _():
        ext[pl.ds(0, TILE), :] = jnp.zeros((TILE, species), ext.dtype)
        crow[0] = jnp.zeros((8, TILE), jnp.float32)
        xin[0] = jnp.zeros((16, TILE), jnp.float32)

    @pl.when(jnp.logical_not(has_right))
    def _():
        ext[pl.ds(ext_rows - TILE, TILE), :] = jnp.zeros((TILE, species), ext.dtype)
        crow[tiles + 1] = jnp.zeros((8, TILE), jnp.float32)
        xin[1] = jnp.zeros((16, TILE), jnp.float32)

    def column(row8):
        return jnp.transpose(jnp.broadcast_to(row8[0:1, :], (TILE, TILE)))

    for e in range(1, tiles + 1):
        ccol[e] = column(crow[e])

    def hit(t, offset):
        wanted = first_tile + t + offset
        found = jnp.int32(0)
        for s in range(nb_ref.shape[1]):
            same = jnp.logical_and(nb_ref[t, s] == wanted, s < cnt_ref[t])
            found = jnp.maximum(found, same.astype(jnp.int32))
        return found.astype(jnp.float32)

    eye = lax.broadcasted_iota(jnp.int32, (TILE, TILE), 0) == lax.broadcasted_iota(
        jnp.int32, (TILE, TILE), 1
    )

    def part(ref, base, i, j):
        return ref[base + i * TILE : base + (i + 1) * TILE, j * TILE : (j + 1) * TILE]

    def own_own(ref, base, k, near, guest=None):
        e = 2 * k
        tiles_g = [[part(ref, base, i, j) for j in range(2)] for i in range(2)]
        rows_inv = []
        cols_inv = []
        for i in range(2):
            diag = jnp.sum(jnp.where(eye, tiles_g[i][i], 0.0), axis=0, keepdims=True)
            inv = jnp.broadcast_to(lax.rsqrt(diag + epsilon), (TILE, TILE))
            col = jnp.transpose(inv) * SCALE
            irow[e + i] = inv[0:8]
            icol[e + i] = col
            rows_inv.append(inv[0:1])
            cols_inv.append(col)
        cc = [ccol[e], ccol[e + 1]]
        w = [[None, None], [None, None]]
        for i in range(2):
            for j in range(2):
                v = jnp.exp2(tiles_g[i][j] * cols_inv[i] * rows_inv[j])
                if i == j and i == guest:
                    w[i][j] = jnp.zeros_like(v)
                elif i == j:
                    w[i][j] = jnp.where(eye, 0.0, v)
                else:
                    w[i][j] = v if near is None else v * near
        for j in range(2):
            if near is None:
                numer, denom = w[j][j] * cc[j], w[j][j]
            else:
                numer, denom = w[0][j] * cc[0] + w[1][j] * cc[1], w[0][j] + w[1][j]
            acc[e + j, 0:8, :] = fold_rows(numer)
            acc[e + j, 8:16, :] = fold_rows(denom)

    def prev_own(ref, base, k, far0, near1, far1):
        e = 2 * k
        r0, r1 = irow[e, 0:1, :], irow[e + 1, 0:1, :]
        w00 = jnp.exp2(part(ref, base, 0, 0) * icol[e - 2] * r0) * far0
        w10 = jnp.exp2(part(ref, base, 1, 0) * icol[e - 1] * r0) * near1
        w11 = jnp.exp2(part(ref, base, 1, 1) * icol[e - 1] * r1) * far1
        cp0, cp1 = ccol[e - 2], ccol[e - 1]
        acc[e, 0:8, :] += fold_rows(w00 * cp0 + w10 * cp1)
        acc[e, 8:16, :] += fold_rows(w00 + w10)
        acc[e + 1, 0:8, :] += fold_rows(w11 * cp1)
        acc[e + 1, 8:16, :] += fold_rows(w11)
        c0, c1 = crow[e, 0:1, :], crow[e + 1, 0:1, :]
        acc[e - 2, 0:8, :] += fold_rows(jnp.transpose(w00 * c0))
        acc[e - 2, 8:16, :] += fold_rows(jnp.transpose(w00))
        acc[e - 1, 0:8, :] += fold_rows(jnp.transpose(w10 * c0 + w11 * c1))
        acc[e - 1, 8:16, :] += fold_rows(jnp.transpose(w10 + w11))

    def pair_rows(k, count=1):
        start = k * PAIR
        if not isinstance(k, int):
            start = pl.multiple_of(start, PAIR)
        return ext[pl.ds(start, count * PAIR), :]

    def block(k, ref):
        ref[...] = gram_dot(pair_rows(k - 1, 2), pair_rows(k))

    def block_post(k, ref):
        own_own(ref, PAIR, k, hit(2 * k - 1, 1))
        prev_own(ref, 0, k, hit(2 * k - 3, 2), hit(2 * k - 2, 1), hit(2 * k - 2, 2))

    def wait_load(k):
        start = pl.multiple_of(k * PAIR, PAIR)
        pltpu.make_async_copy(
            occ_hbm.at[pl.ds(start - TILE, PAIR)], ext.at[pl.ds(start, PAIR)], load_sem.at[k]
        ).wait()

    load(1).wait()
    gram_b[0:PAIR, :] = gram_dot(pair_rows(1), pair_rows(1))
    load(2).wait()
    block(2, gram_a)
    own_own(gram_b, 0, 1, hit(1, 1))

    def two(i, carry):
        k = 2 * i + 3
        wait_load(k)
        block(k, gram_b)
        block_post(k - 1, gram_a)
        wait_load(k + 1)
        block(k + 1, gram_a)
        block_post(k, gram_b)
        return carry

    steps = (last - 3) // 2
    lax.fori_loop(0, steps, two, 0)
    tail = 2 * steps + 3
    current = gram_a
    for k in range(tail, last):
        other = gram_b if current is gram_a else gram_a
        load(k).wait()
        block(k, other)
        block_post(k - 1, current)
        current = other

    load(0).wait()
    load(last).wait()
    other = gram_b if current is gram_a else gram_a

    @pl.when(has_left)
    def _():
        halo_r.wait_recv()
        cond_r.wait_recv()

    @pl.when(has_right)
    def _():
        halo_l.wait_recv()
        cond_l.wait_recv()

    ccol[0] = column(crow[0])
    ccol[tiles + 1] = column(crow[tiles + 1])
    other[0:PAIR, :] = gram_dot(pair_rows(0), pair_rows(0))
    other[PAIR:, :] = gram_dot(pair_rows(0), pair_rows(1))
    block_post(last - 1, current)
    block(last, current)
    own_own(other, 0, 0, hit(0, -1), 0)
    prev_own(other, PAIR, 1, hit(1, -2), hit(0, 1), hit(0, 2))
    own_own(current, PAIR, last, None, 1)
    prev_own(current, 0, last, hit(tiles - 3, 2), hit(tiles - 2, 1), hit(tiles - 2, 2))

    @pl.when(has_right)
    def _():
        acc_r.start()

    @pl.when(has_left)
    def _():
        acc_l.start()

    line = lax.broadcasted_iota(jnp.int32, (16, TILE), 0)

    def finish(t, extra):
        e = t + 1
        total = acc[e]
        if extra is not None:
            total = total + xin[extra]
        numer = jnp.sum(total[0:8], axis=0, keepdims=True)
        denom = jnp.sum(total[8:16], axis=0, keepdims=True)
        eff = crow[e, 0:1, :] * numer / denom
        eff_ref[t : t + 1, :] = eff
        both = jnp.where(line == 0, eff, jnp.where(line == 1, 1.0, 0.0))
        wl[:, t * TILE : (t + 1) * TILE] = both.astype(jnp.bfloat16)

    for t in range(1, tiles - 1):
        finish(t, None)

    step = 512 if species % 512 == 0 else TILE

    def inner(i, carry):
        cols = pl.ds(pl.multiple_of(i * step, step), step)
        got = jnp.dot(
            wl[:, TILE : rows - TILE], ext[PAIR : rows, cols], preferred_element_type=jnp.float32
        )
        sums_ref[:, cols] = got[0:8]
        return carry

    lax.fori_loop(0, species // step, inner, 0)

    @pl.when(has_left)
    def _():
        acc_r.wait_recv()

    @pl.when(has_right)
    def _():
        acc_l.wait_recv()

    finish(0, 0)
    finish(tiles - 1, 1)

    def outer(i, carry):
        cols = pl.ds(pl.multiple_of(i * step, step), step)
        got = jnp.dot(
            wl[:, 0:TILE], ext[TILE:PAIR, cols], preferred_element_type=jnp.float32
        ) + jnp.dot(
            wl[:, rows - TILE : rows], ext[rows : rows + TILE, cols],
            preferred_element_type=jnp.float32,
        )
        sums_ref[:, cols] += got[0:8]
        return carry

    lax.fori_loop(0, species // step, outer, 0)

    @pl.when(has_right)
    def _():
        halo_r.wait_send()
        cond_r.wait_send()
        acc_r.wait_send()

    @pl.when(has_left)
    def _():
        halo_l.wait_send()
        cond_l.wait_send()
        acc_l.wait_send()


def exchange_kernel(n_cell, devices, per, wide, sums_ref, out_ref, got, send_sem, recv_sem):
    me = lax.axis_index("grp") * n_cell + lax.axis_index("cell")
    mesh_id = pl.DeviceIdType.MESH

    def block_of(owner):
        return sums_ref.at[:, pl.ds(pl.multiple_of((owner * per) // wide * wide, wide), wide)]

    def peer(j):
        owner = lax.rem(me + j, devices)
        return owner, (owner // n_cell, lax.rem(owner, n_cell))

    def copy(j):
        owner, target = peer(j)
        return pltpu.make_async_remote_copy(
            src_ref=block_of(owner), dst_ref=got.at[j], send_sem=send_sem.at[j],
            recv_sem=recv_sem.at[j], device_id=target, device_id_type=mesh_id,
        )

    barrier = pltpu.get_barrier_semaphore()

    def greet(j, carry):
        pl.semaphore_signal(barrier, inc=1, device_id=peer(j)[1], device_id_type=mesh_id)
        return carry

    def send(j, carry):
        copy(j).start()
        return carry

    def finish(j, carry):
        copy(j).wait()
        return carry

    lax.fori_loop(1, devices, greet, 0)
    pl.semaphore_wait(barrier, devices - 1)
    lax.fori_loop(1, devices, send, 0)
    got[0] = block_of(me)[...]
    lax.fori_loop(1, devices, finish, 0)
    out_ref[...] = jnp.sum(got[...], axis=0)


def per_device(n_cell, occurrence, condition, neighbours, pair_count):
    tiles = pair_count.shape[0]
    rows, species = occurrence.shape
    cond = condition.astype(jnp.float32).reshape(tiles, TILE)
    vmem = pl.BlockSpec(memory_space=pltpu.VMEM)
    smem = pl.BlockSpec(memory_space=pltpu.SMEM)
    effective, sums = pl.pallas_call(
        functools.partial(main_kernel, n_cell, tiles),
        out_shape=(
            jax.ShapeDtypeStruct((tiles, TILE), jnp.float32),
            jax.ShapeDtypeStruct((8, species), jnp.float32),
        ),
        in_specs=[pl.BlockSpec(memory_space=pl.ANY), vmem, smem, smem],
        out_specs=(vmem, vmem),
        scratch_shapes=[
            pltpu.VMEM((rows + PAIR, species), jnp.bfloat16),
            pltpu.VMEM((2 * PAIR, PAIR), jnp.float32),
            pltpu.VMEM((2 * PAIR, PAIR), jnp.float32),
            pltpu.VMEM((tiles + 2, 8, TILE), jnp.float32),
            pltpu.VMEM((tiles + 2, TILE, TILE), jnp.float32),
            pltpu.VMEM((tiles + 2, 8, TILE), jnp.float32),
            pltpu.VMEM((tiles + 2, TILE, TILE), jnp.float32),
            pltpu.VMEM((tiles + 2, 16, TILE), jnp.float32),
            pltpu.VMEM((2, 16, TILE), jnp.float32),
            pltpu.VMEM((16, rows), jnp.bfloat16),
            pltpu.SemaphoreType.DMA((tiles // 2 + 1,)),
            pltpu.SemaphoreType.DMA((2,)),
            pltpu.SemaphoreType.DMA((2,)),
            pltpu.SemaphoreType.DMA((2,)),
            pltpu.SemaphoreType.DMA((2,)),
            pltpu.SemaphoreType.DMA((2,)),
            pltpu.SemaphoreType.DMA((2,)),
        ],
        compiler_params=pltpu.CompilerParams(
            collective_id=0, has_side_effects=True, vmem_limit_bytes=56 * 2**20
        ),
    )(occurrence, cond, neighbours, pair_count)
    devices = lax.axis_size(("grp", "cell"))
    per = species // devices
    wide = max(per, TILE)
    totals = pl.pallas_call(
        functools.partial(exchange_kernel, n_cell, devices, per, wide),
        out_shape=jax.ShapeDtypeStruct((8, wide), jnp.float32),
        in_specs=[vmem],
        out_specs=vmem,
        scratch_shapes=[
            pltpu.VMEM((devices, 8, wide), jnp.float32),
            pltpu.SemaphoreType.DMA((devices,)),
            pltpu.SemaphoreType.DMA((devices,)),
        ],
        compiler_params=pltpu.CompilerParams(collective_id=1, has_side_effects=True),
    )(sums)
    if per < wide:
        offset = lax.rem(lax.axis_index(("grp", "cell")) * per, wide)
        totals = lax.dynamic_slice_in_dim(totals, offset, per, axis=1)
    persistence = (totals[0] / totals[1]) ** exponent
    return effective.reshape(rows), persistence


def solution(mesh):
    return jax.shard_map(
        functools.partial(per_device, mesh.shape["cell"]),
        mesh=mesh,
        in_specs=(
            P(("grp", "cell"), None),
            P(("grp", "cell")),
            P(("grp", "cell"), None),
            P(("grp", "cell")),
        ),
        out_specs=(P(("grp", "cell")), P(("grp", "cell"))),
        check_vma=False,
    )
```
